32 devices in a mesh: ctx: 16 (over z, y, core), grp: 2 (over x).
Axes of the slice: x: 2, y: 2, z: 4, core: 2. Of those that a mesh axis runs over, the one named last changes fastest.
Arguments:
- queries: bfloat16 [2048, 1024], P('ctx', 'grp'), may hold values from -6 to 6
- keys: bfloat16 [2048, 1024], P('ctx', 'grp'), may hold values from -6 to 6
- values: bfloat16 [2048, 1024], P('ctx', 'grp'), may hold values from -6 to 6
- block_order: int32 [32], replicated, may hold values from 0 to 31, each once
- token_ids: int32 [2048], P('ctx'), may hold values from 0 to 511
- stream_table: bfloat16 [4, 512, 2048], P(None, None, 'grp'), may hold values from -70 to 70
- short_filter: float32 [3, 7, 2048], P(None, None, 'grp'), may hold values from -2 to 2
- long_filter: bfloat16 [128, 128], P('grp'), may hold values from -0.5 to 0.5
- norm_gain: float32 [2048], P('grp'), may hold values from 0.1 to 1.9
Outputs:
- attended: bfloat16 [2048, 1024], P('ctx', 'grp')
- hyena_out: bfloat16 [2048, 2048], P('ctx', 'grp')
The draws below stay inside these ranges and needn't reach their ends.
All inputs are finite; a program needn't handle non-finite values.
Results may differ from the reference program's by a relative error of at most 0.004.
Values may be sent and summed in bfloat16 or wider, within the bound.
A program may use at most 128 MiB of HBM per device.

```python
import math
import jax
import jax.numpy as jnp
from jax import lax

HD = 128
HEADS = 8
CHANNELS = 2048
GSIZE = 16
FILTERS = 128
TAPS = 128
SHORT = 7
VOCAB = 512
TOK_DEV = 128
SEQ = 2048
N_CTX = 16


def base_draw(key, salt):
    inner = jax.random.fold_in(key, salt)
    return jnp.clip(1.6 * jax.random.normal(inner, (SEQ, HEADS * HD), jnp.float32), -6.0, 6.0)


def draw_queries(key, part):
    result = base_draw(key, 11)
    return result.astype(jnp.bfloat16)


def draw_keys(key, part):
    result = base_draw(key, 12)
    return result.astype(jnp.bfloat16)


def draw_stream_table(key, part):
    picks = jax.random.split(jax.random.fold_in(key, 907), 2)
    column = jnp.arange(CHANNELS, dtype=jnp.float32) / CHANNELS
    row_level = jax.random.uniform(picks[1], (1, VOCAB, 1), jnp.float32)
    result = jnp.clip(jax.random.normal(picks[0], (4, VOCAB, CHANNELS), jnp.float32), -4.0, 4.0)
    ramp = 0.2 * 10.0 ** column
    scaled = result * ramp[None, None, :] * 10.0 ** (row_level - 0.5)
    stream = jnp.arange(4)[:, None, None]
    return jnp.where(stream == 0, scaled, result).astype(jnp.bfloat16)


def touch_ends(array, rng, smallest, high):
    longest = array.shape.index(max(array.shape))
    spots = []
    for shift in (0, 1):
        where = [jax.random.randint(jax.random.fold_in(rng, axis), (), 0, length) for axis, length in enumerate(array.shape)]
        where[longest] = (where[longest] + shift) % array.shape[longest]
        spots.append(tuple(where))
    return array.at[spots[0]].set(smallest).at[spots[1]].set(high)


def levels(key, extent, pieces, smallest, top_value):
    factor_of = 1.0
    for axis_at, shards_of in pieces:
        steps = jax.random.uniform(jax.random.fold_in(jax.random.fold_in(key, 6), axis_at), (shards_of,), jnp.float32, smallest / len(pieces), top_value / len(pieces))
        factor_of = factor_of * jnp.repeat(jnp.exp(steps), extent[axis_at] // shards_of).reshape((-1,) + (1,) * (len(extent) - 1 - axis_at))
    return factor_of


def scatter_about(own_key, extent, width, reach, shards=(), kind=jnp.bfloat16):
    drawn = jax.random.normal(own_key, extent, jnp.float32) * width
    if len(shards) > 0:
        drawn = levels(own_key, extent, shards, -0.22, 0.18) * drawn
    return jnp.clip(drawn, min=-reach, max=reach).astype(kind)


def setup_inputs(seed: int = 0) -> dict:
    streams_of = jax.random.split(jax.random.key(seed), 10)
    queries = draw_queries(jax.random.fold_in(streams_of[9], 71), 0)
    keys = draw_keys(jax.random.fold_in(streams_of[9], 71), 0)
    values = scatter_about(streams_of[2], (SEQ, HEADS * HD), 1.0, 6.0, ((0, 16), (1, 2)))
    block_order = jax.random.permutation(streams_of[3], 2 * N_CTX).astype(jnp.int32)
    token_ids = touch_ends(jax.random.randint(streams_of[4], (SEQ,), 0, VOCAB), jax.random.fold_in(streams_of[4], 1), 0, VOCAB - 1).astype(jnp.int32)
    stream_table = draw_stream_table(jax.random.fold_in(streams_of[9], 71), 0)
    short_filter = scatter_about(streams_of[6], (3, SHORT, CHANNELS), SHORT ** -0.5, 2.0, ((2, 2),), jnp.float32)
    long_filter = scatter_about(streams_of[7], (FILTERS, TAPS), TAPS ** -0.5, 0.5, ((0, 2),))
    norm_gain = jnp.clip(1.0 + 0.18 * jax.random.normal(streams_of[8], (CHANNELS,), jnp.float32), 0.1, 1.9)
    return dict(queries=queries, keys=keys, values=values, block_order=block_order, token_ids=token_ids, stream_table=stream_table, short_filter=short_filter, long_filter=long_filter, norm_gain=norm_gain)


def reference(queries, keys, values, block_order, token_ids, stream_table, short_filter, long_filter, norm_gain):
    seq_len = queries.shape[0]
    half_rows = TOK_DEV // 2
    row_index = jnp.arange(seq_len, dtype=jnp.int32)
    slot = (2 * (row_index // TOK_DEV) + row_index % TOK_DEV // half_rows).astype(jnp.int32)
    position = block_order[slot] * half_rows + row_index % half_rows
    score_scale = 1.0 / math.sqrt(HD)
    block_rows = math.gcd(seq_len, 1024)
    query_heads = queries.reshape(seq_len, HEADS, HD).transpose(1, 0, 2)
    key_heads = keys.reshape(seq_len, HEADS, HD).transpose(1, 0, 2)
    value_heads = values.reshape(seq_len, HEADS, HD).transpose(1, 0, 2)

    def one_head(operands):
        head_q, head_k, head_v = operands

        def one_block(offset):
            block_q = lax.dynamic_slice_in_dim(head_q, offset, block_rows, 0)
            block_pos = lax.dynamic_slice_in_dim(position, offset, block_rows, 0)
            scores = jnp.dot(block_q, head_k.T, preferred_element_type=jnp.float32) * score_scale
            visible = position[None, :] <= block_pos[:, None]
            scores = jnp.where(visible, scores, -1e+30)
            row_peak = lax.optimization_barrier(jnp.max(scores, axis=1, keepdims=True))
            weights = jnp.where(visible, jnp.exp(scores - row_peak), 0.0)
            row_total = lax.optimization_barrier(jnp.sum(weights, axis=1, keepdims=True))
            summed = jnp.dot(weights.astype(jnp.bfloat16), head_v, preferred_element_type=jnp.float32)
            return (summed / row_total).astype(jnp.bfloat16)
        offsets = (jnp.arange(seq_len // block_rows) * block_rows).astype(jnp.int32)
        return lax.map(one_block, offsets).reshape(seq_len, HD)
    attended = lax.map(one_head, (query_heads, key_heads, value_heads))
    attended = attended.transpose(1, 0, 2).reshape(seq_len, HEADS * HD)
    feats = stream_table[:, token_ids, :]
    shorts = []
    for stream in range(3):
        source = feats[stream + 1].astype(jnp.float32)
        padded = jnp.pad(source, ((SHORT - 1, 0), (0, 0)))
        running = jnp.zeros((seq_len, CHANNELS), jnp.float32)
        for lag_step in range(SHORT):
            running = running + short_filter[stream, lag_step][None, :] * padded[SHORT - 1 - lag_step:SHORT - 1 - lag_step + seq_len]
        shorts.append(running)
    product = (shorts[0] * shorts[2]).astype(jnp.bfloat16)
    spread = jnp.repeat(long_filter.astype(jnp.float32), GSIZE, axis=0).T
    product_pad = jnp.pad(product.astype(jnp.float32), ((TAPS - 1, 0), (0, 0)))

    def add_tap(tap_index, running):
        window = lax.dynamic_slice_in_dim(product_pad, TAPS - 1 - tap_index, seq_len, 0)
        tap_row = lax.dynamic_slice_in_dim(spread, tap_index, 1, 0)
        return running + tap_row * window
    convolved = lax.fori_loop(0, TAPS, add_tap, jnp.zeros((seq_len, CHANNELS), jnp.float32))
    mixed = feats[0].astype(jnp.float32) + shorts[1] * convolved
    mean_square = lax.optimization_barrier(jnp.mean(mixed * mixed, axis=1, keepdims=True))
    hyena_out = (mixed * norm_gain[None, :] / jnp.sqrt(mean_square + 1e-06)).astype(jnp.bfloat16)
    return (attended, hyena_out)
```

```python
import functools
import math

import jax
import jax.numpy as jnp
from jax import lax
from jax.experimental import pallas as pl
from jax.experimental.pallas import tpu as pltpu
from jax.sharding import PartitionSpec as P

HD = 128
MESH = pl.DeviceIdType.MESH
neg_fill = -1e30
eps_norm = 1e-06
F32 = jnp.float32
BF16 = jnp.bfloat16


def ceil_to(value, unit):
    return -(-value // unit) * unit


def kernel(
    sizes,
    order_ref,
    q_ref,
    k_ref,
    v_ref,
    ids_ref,
    table_ref,
    short_ref,
    long_ref,
    gain_ref,
    att_ref,
    hy_ref,
    kbuf,
    vbuf,
    qbuf,
    obuf,
    oland,
    ids_buf,
    table_buf,
    hot,
    feat_a,
    feat_b,
    feat_c,
    prod,
    taps_buf,
    mixed,
    squares,
    peak,
    total,
    acc,
    own_sem,
    pair_send,
    pair_recv,
    ids_send,
    ids_recv,
    ring_send,
    ring_recv,
    table_sem,
    sq_send,
    sq_recv,
    out_send,
    out_recv,
):
    n_ctx, n_grp, tile = sizes
    rows, width = q_ref.shape
    half_width = width // 2
    heads = half_width // HD
    half_rows = rows // 2
    channels = table_ref.shape[2]
    vocab = table_ref.shape[1]
    short_taps = short_ref.shape[1]
    groups, taps = long_ref.shape
    group_size = channels // groups
    units = channels // tile
    lead = hot.shape[0] - rows
    behind = lead - rows
    chips = n_ctx // 2
    far = chips // 2

    me = lax.axis_index("ctx")
    my_grp = lax.axis_index("grp")
    chip = me // 2
    core = me % 2

    def ring_of(c):
        return jnp.where(c % 2 == 0, c // 2, chips - 1 - c // 2)

    def chip_at(place):
        return jnp.where(place < far, 2 * place, 2 * (chips - 1 - place) + 1)

    place = ring_of(chip)
    sibling = chip * 2 + (1 - core)
    right = chip_at(lax.rem(place + 1, chips)) * 2 + core
    left = chip_at(lax.rem(place + chips - 1, chips)) * 2 + core
    after = [lax.rem(me + d, n_ctx) for d in (1, 2)]
    before = [lax.rem(me + n_ctx - d, n_ctx) for d in (1, 2)]
    peers = [lax.rem(my_grp + d, n_grp) for d in range(1, n_grp)]

    barrier = pltpu.get_barrier_semaphore()
    greet = [(t, my_grp) for t in [sibling, right, left] + after + before]
    greet += [(me, g) for g in peers]
    for target in greet:
        pl.semaphore_signal(barrier, inc=1, device_id=target, device_id_type=MESH)

    table_copies = []
    for j in range(units):
        cols = pl.ds(j * tile, tile)
        table_copies.append(
            pltpu.make_async_copy(
                table_ref.at[:, :, cols], table_buf.at[j], table_sem.at[j]
            )
        )
        table_copies[-1].start()
    mine = pl.ds(pl.multiple_of(core * half_width, half_width), half_width)
    theirs = pl.ds(pl.multiple_of((1 - core) * half_width, half_width), half_width)
    my_rows = pl.ds(pl.multiple_of(core * rows, rows), rows)
    pairs = ((k_ref, kbuf.at[0]), (v_ref, vbuf.at[0]), (q_ref, qbuf))
    own_copies = []
    for i, (src, dst) in enumerate(pairs):
        own_copies.append(
            pltpu.make_async_copy(src.at[:, mine], dst.at[my_rows, :], own_sem.at[i])
        )
        own_copies[-1].start()

    pl.semaphore_wait(barrier, len(greet))

    pair_copies = []
    for i, (src, dst) in enumerate(pairs):
        pair_copies.append(
            pltpu.make_async_remote_copy(
                src_ref=src.at[:, theirs],
                dst_ref=dst.at[my_rows, :],
                send_sem=pair_send.at[i],
                recv_sem=pair_recv.at[i],
                device_id=(sibling, my_grp),
                device_id_type=MESH,
            )
        )
        pair_copies[-1].start()
    ids_copies = []
    for i in range(2):
        ids_copies.append(
            pltpu.make_async_remote_copy(
                src_ref=ids_ref,
                dst_ref=ids_buf.at[i],
                send_sem=ids_send.at[i],
                recv_sem=ids_recv.at[i],
                device_id=(after[i], my_grp),
                device_id_type=MESH,
            )
        )
        ids_copies[-1].start()

    def ring_copy(to_right, is_key, step):
        buf = kbuf if is_key else vbuf
        if to_right:
            src, dst = step - 1, step
        else:
            src, dst = (chips - step + 1) % chips, chips - step
        slot = (0 if to_right else 1, 0 if is_key else 1, step - 1)
        return pltpu.make_async_remote_copy(
            src_ref=buf.at[src],
            dst_ref=buf.at[dst],
            send_sem=ring_send.at[slot],
            recv_sem=ring_recv.at[slot],
            device_id=(right if to_right else left, my_grp),
            device_id_type=MESH,
        )

    for i in range(2):
        own_copies[i].wait()
        pair_copies[i].wait_recv()
        ring_copy(True, i == 0, 1).start() if i == 0 or far > 1 else None
        ring_copy(False, i == 0, 1).start() if i == 1 or far > 1 else None

    def pass_on(step, first):
        last = step + 1 == far
        for to_right in (True, False):
            is_key = to_right == first
            ring_copy(to_right, is_key, step).wait_recv()
            if first or not last:
                ring_copy(to_right, is_key, step + 1).start()

    anti = lax.broadcasted_iota(jnp.int32, (taps, rows + taps), 1) + lax.broadcasted_iota(
        jnp.int32, (taps, rows + taps), 0
    )
    anti = jnp.where(anti == taps, 1.0, 0.0).astype(BF16)
    taps_buf[...] = jnp.dot(long_ref[...], anti, preferred_element_type=F32)

    for copy in ids_copies:
        copy.wait_recv()
    first_row = me * rows

    def one_hot(row_ids, offset):
        down = jnp.transpose(jnp.broadcast_to(row_ids, (HD, rows)))
        spot = lax.broadcasted_iota(jnp.int32, (rows, HD), 0) + (first_row + offset)
        down = jnp.where(spot >= 0, down, -1)
        lane = lax.broadcasted_iota(jnp.int32, (rows, HD), 1)
        parts = [
            jnp.where(down == lane + b * HD, 1.0, 0.0).astype(BF16) for b in range(vocab // HD)
        ]
        return jnp.concatenate(parts, axis=1)

    hot[0:behind, :] = one_hot(ids_buf[1], -2 * rows)[rows - behind :, :]
    hot[behind : behind + rows, :] = one_hot(ids_buf[0], -rows)
    hot[behind + rows :, :] = one_hot(ids_ref[...], 0)

    tail = rows + 16

    def short_rows(feat, stream, base, count, lanes, cols):
        out = None
        for k in range(short_taps):
            term = short_ref[stream, pl.ds(k, 1), cols] * feat[
                pl.ds(base - k, count), lanes
            ]
            out = term if out is None else out + term
        return out

    def hyena_unit(j, done):
        table_copies[j].wait()
        feat_a[...] = jnp.dot(hot[...], table_buf[j, 1], preferred_element_type=F32)
        feat_c[...] = jnp.dot(hot[...], table_buf[j, 3], preferred_element_type=F32)
        feat_b[...] = jnp.dot(
            hot[lead - 16 :, :], table_buf[j, 2], preferred_element_type=F32
        )
        residual = jnp.dot(hot[lead:, :], table_buf[j, 0], preferred_element_type=F32)
        mixed[:, j * tile : (j + 1) * tile] = residual
        step_rows = 64
        for sub in range(tile // HD):
            lanes = slice(sub * HD, (sub + 1) * HD)
            cols = slice(j * tile + sub * HD, j * tile + (sub + 1) * HD)
            for r in range(0, taps + rows, step_rows):
                base = lead - taps + r
                one = short_rows(feat_a, 0, base, step_rows, lanes, cols)
                three = short_rows(feat_c, 2, base, step_rows, lanes, cols)
                prod[r : r + step_rows, lanes] = (one * three).astype(BF16)
        done()
        for sub in range(tile // HD):
            lanes = slice(sub * HD, (sub + 1) * HD)
            cols = slice(j * tile + sub * HD, j * tile + (sub + 1) * HD)
            block = prod[:, lanes]
            lane_group = lax.broadcasted_iota(jnp.int32, (rows, HD), 1) // group_size
            per_sub = HD // group_size
            first_group = (j * tile + sub * HD) // group_size

            def add_group(g, conv):
                line = taps_buf[pl.ds(first_group + g, 1), :]
                wide = jnp.broadcast_to(line, (rows, rows + taps))
                band = pltpu.roll(wide, 0, 1, stride=1, stride_axis=0).astype(BF16)
                part = jnp.dot(band, block, preferred_element_type=F32)
                return jnp.where(lane_group == g, part, conv)

            conv = lax.fori_loop(
                0, per_sub, add_group, jnp.zeros((rows, HD), F32), unroll=True
            )
            two = short_rows(feat_b, 1, 16, rows, lanes, cols)
            whole = mixed[:, cols] + two * conv
            mixed[:, cols] = whole
            square = whole * whole
            if j == 0 and sub == 0:
                squares[0] = square
            else:
                squares[0] = squares[0] + square

    def positions(of_chip, shape, dim):
        at = lax.broadcasted_iota(jnp.int32, shape, dim)
        piece = at // half_rows
        start = jnp.full(shape, order_ref[of_chip * 4], jnp.int32)
        for b in range(1, 4):
            start = jnp.where(piece == b, order_ref[of_chip * 4 + b], start)
        return start * half_rows + at % half_rows

    scale = 1.0 / math.sqrt(HD)

    def attend(slot, start):
        owner = chip_at(lax.rem(place + chips - slot, chips))
        key_pos = positions(owner, (1, 2 * rows), 1)
        query_pos = positions(chip, (2 * rows, 1), 0)
        visible = key_pos <= query_pos
        for head in range(heads):
            cols = slice(head * HD, (head + 1) * HD)
            scores = lax.dot_general(
                qbuf[:, cols],
                kbuf[slot, :, cols],
                (((1,), (1,)), ((), ())),
                preferred_element_type=F32,
            )
            scores = jnp.where(visible, scores * scale, neg_fill)
            top = jnp.max(scores, axis=1, keepdims=True)
            if not start:
                old = peak[head]
                top = jnp.maximum(old, top)
            weights = jnp.where(visible, jnp.exp(scores - top), 0.0)
            mass = jnp.sum(weights, axis=1, keepdims=True)
            summed = jnp.dot(
                weights.astype(BF16), vbuf[slot, :, cols], preferred_element_type=F32
            )
            if not start:
                shrink = jnp.exp(old - top)
                mass = total[head] * shrink + mass
                summed = acc[head] * shrink + summed
            peak[head] = top
            total[head] = mass
            acc[head] = summed

    events = [(s, f) for s in range(1, far) for f in (True, False)]
    passed = []

    def next_event():
        if events:
            step, first = events.pop(0)
            pass_on(step, first)
            if not first:
                passed.append(step)

    def nothing():
        return None

    for j in range(units):
        hyena_unit(j, next_event if j % 2 == 0 else nothing)

    sq_copies = []
    for i, g in enumerate(peers):
        sq_copies.append(
            pltpu.make_async_remote_copy(
                src_ref=squares.at[0],
                dst_ref=squares.at[i + 1],
                send_sem=sq_send.at[i],
                recv_sem=sq_recv.at[i],
                device_id=(me, g),
                device_id_type=MESH,
            )
        )
        sq_copies[-1].start()

    next_event()
    own_copies[2].wait()
    pair_copies[2].wait_recv()
    attend(0, True)
    while events:
        for step in passed:
            attend(step, False)
            attend(chips - step, False)
        passed.clear()
        next_event()

    for copy in sq_copies:
        copy.wait_recv()
    sum_sq = squares[0]
    for i in range(len(peers)):
        sum_sq = sum_sq + squares[i + 1]
    mean = jnp.sum(sum_sq, axis=1, keepdims=True) / (channels * n_grp)
    inverse = lax.rsqrt(mean + eps_norm)
    hy_ref[...] = (mixed[...] * gain_ref[...] * inverse).astype(BF16)
    for step in passed:
        attend(step, False)
        attend(chips - step, False)

    ring_copy(True, True, far).wait_recv()
    ring_copy(False, False, far).wait_recv()
    attend(far, False)

    for head in range(heads):
        cols = slice(head * HD, (head + 1) * HD)
        obuf[:, cols] = (acc[head] / total[head]).astype(BF16)
    their_rows = pl.ds(pl.multiple_of((1 - core) * rows, rows), rows)
    back = pltpu.make_async_remote_copy(
        src_ref=obuf.at[their_rows, :],
        dst_ref=oland,
        send_sem=out_send,
        recv_sem=out_recv,
        device_id=(sibling, my_grp),
        device_id_type=MESH,
    )
    back.start()
    for copy in pair_copies + ids_copies + sq_copies:
        copy.wait_send()
    for step in range(1, far + 1):
        for to_right in (True, False):
            for is_key in (True, False):
                if step < far or to_right == is_key:
                    ring_copy(to_right, is_key, step).wait_send()
    kept = obuf[my_rows, :]
    back.wait()
    got = oland[...]
    att_ref[:, :half_width] = jnp.where(core == 0, kept, got)
    att_ref[:, half_width:] = jnp.where(core == 0, got, kept)


def body(
    n_ctx,
    n_grp,
    queries,
    keys,
    values,
    block_order,
    token_ids,
    stream_table,
    short_filter,
    long_filter,
    norm_gain,
):
    rows, width = queries.shape
    half_width = width // 2
    heads = half_width // HD
    channels = stream_table.shape[2]
    vocab = stream_table.shape[1]
    groups, taps = long_filter.shape
    lead = ceil_to(taps - 1 + short_filter.shape[1] - 1, 16)
    tile = math.gcd(channels, 256)
    units = channels // tile
    chips = n_ctx // 2
    far = chips // 2
    vmem = pl.BlockSpec(memory_space=pltpu.VMEM)
    dma = pltpu.SemaphoreType.DMA
    return pl.pallas_call(
        functools.partial(kernel, (n_ctx, n_grp, tile)),
        out_shape=(
            jax.ShapeDtypeStruct((rows, width), BF16),
            jax.ShapeDtypeStruct((rows, channels), BF16),
        ),
        in_specs=[
            pl.BlockSpec(memory_space=pltpu.SMEM),
            vmem,
            vmem,
            vmem,
            vmem,
            pl.BlockSpec(memory_space=pl.ANY),
            vmem,
            vmem,
            vmem,
        ],
        out_specs=(vmem, vmem),
        scratch_shapes=[
            pltpu.VMEM((chips, 2 * rows, half_width), BF16),
            pltpu.VMEM((chips, 2 * rows, half_width), BF16),
            pltpu.VMEM((2 * rows, half_width), BF16),
            pltpu.VMEM((2 * rows, half_width), BF16),
            pltpu.VMEM((rows, half_width), BF16),
            pltpu.VMEM((2, 1, rows), jnp.int32),
            pltpu.VMEM((units, 4, vocab, tile), BF16),
            pltpu.VMEM((lead + rows, vocab), BF16),
            pltpu.VMEM((lead + rows, tile), F32),
            pltpu.VMEM((rows + 16, tile), F32),
            pltpu.VMEM((lead + rows, tile), F32),
            pltpu.VMEM((rows + taps, tile), BF16),
            pltpu.VMEM((groups, rows + taps), F32),
            pltpu.VMEM((rows, channels), F32),
            pltpu.VMEM((n_grp, rows, HD), F32),
            pltpu.VMEM((heads, 2 * rows, 1), F32),
            pltpu.VMEM((heads, 2 * rows, 1), F32),
            pltpu.VMEM((heads, 2 * rows, HD), F32),
            dma((3,)),
            dma((3,)),
            dma((3,)),
            dma((2,)),
            dma((2,)),
            dma((2, 2, far)),
            dma((2, 2, far)),
            dma((units,)),
            dma((max(n_grp - 1, 1),)),
            dma((max(n_grp - 1, 1),)),
            dma,
            dma,
        ],
        compiler_params=pltpu.CompilerParams(
            collective_id=0, has_side_effects=True, vmem_limit_bytes=48 * 1024 * 1024
        ),
    )(
        block_order,
        queries,
        keys,
        values,
        token_ids.reshape(1, rows),
        stream_table,
        short_filter,
        long_filter,
        norm_gain.reshape(1, channels),
    )


def solution(mesh):
    placed = (
        P("ctx", "grp"),
        P("ctx", "grp"),
        P("ctx", "grp"),
        P(),
        P("ctx"),
        P(None, None, "grp"),
        P(None, None, "grp"),
        P("grp", None),
        P("grp"),
    )
    return jax.shard_map(
        functools.partial(body, mesh.shape["ctx"], mesh.shape["grp"]),
        mesh=mesh,
        in_specs=placed,
        out_specs=(P("ctx", "grp"), P("ctx", "grp")),
        check_vma=False,
    )
```

```python
import functools
import math

import jax
import jax.numpy as jnp
from jax import lax
from jax.experimental import pallas as pl
from jax.experimental.pallas import tpu as pltpu
from jax.sharding import PartitionSpec as P

HD = 128
MESH = pl.DeviceIdType.MESH
neg_fill = -1e30
eps_norm = 1e-06
F32 = jnp.float32
BF16 = jnp.bfloat16


def ceil_to(value, unit):
    return -(-value // unit) * unit


def kernel(
    sizes,
    order_in,
    q_ref,
    k_ref,
    v_ref,
    ids_in,
    table_ref,
    short_in,
    long_in,
    gain_in,
    att_ref,
    hy_ref,
    order_ref,
    ids_ref,
    short_ref,
    long_ref,
    gain_ref,
    small_sem,
    kbuf,
    vbuf,
    qbuf,
    obuf,
    oland,
    ids_buf,
    table_buf,
    hot,
    feat_a,
    feat_b,
    feat_c,
    prod,
    taps_buf,
    mixed,
    squares,
    peak,
    total,
    acc,
    own_sem,
    pair_send,
    pair_recv,
    ids_send,
    ids_recv,
    ring_send,
    ring_recv,
    table_sem,
    sq_send,
    sq_recv,
    out_send,
    out_recv,
):
    n_ctx, n_grp, tile = sizes
    rows, width = q_ref.shape
    half_width = width // 2
    heads = half_width // HD
    half_rows = rows // 2
    channels = table_ref.shape[2]
    vocab = table_ref.shape[1]
    short_taps = short_ref.shape[1]
    groups, taps = long_ref.shape
    group_size = channels // groups
    units = channels // tile
    lead = hot.shape[0] - rows
    behind = lead - rows
    chips = n_ctx // 2
    far = chips // 2

    me = lax.axis_index("ctx")
    my_grp = lax.axis_index("grp")
    chip = me // 2
    core = me % 2

    def ring_of(c):
        return jnp.where(c % 2 == 0, c // 2, chips - 1 - c // 2)

    def chip_at(place):
        return jnp.where(place < far, 2 * place, 2 * (chips - 1 - place) + 1)

    place = ring_of(chip)
    sibling = chip * 2 + (1 - core)
    right = chip_at(lax.rem(place + 1, chips)) * 2 + core
    left = chip_at(lax.rem(place + chips - 1, chips)) * 2 + core
    after = [lax.rem(me + d, n_ctx) for d in (1, 2)]
    before = [lax.rem(me + n_ctx - d, n_ctx) for d in (1, 2)]
    peers = [lax.rem(my_grp + d, n_grp) for d in range(1, n_grp)]

    barrier = pltpu.get_barrier_semaphore()
    greet = [(t, my_grp) for t in [sibling, right, left] + after + before]
    greet += [(me, g) for g in peers]
    for target in greet:
        pl.semaphore_signal(barrier, inc=1, device_id=target, device_id_type=MESH)

    mine = pl.ds(pl.multiple_of(core * half_width, half_width), half_width)
    theirs = pl.ds(pl.multiple_of((1 - core) * half_width, half_width), half_width)
    my_rows = pl.ds(pl.multiple_of(core * rows, rows), rows)
    pairs = ((k_ref, kbuf.at[0]), (v_ref, vbuf.at[0]), (q_ref, qbuf))
    own_copies = []
    for i, (src, dst) in enumerate(pairs):
        own_copies.append(
            pltpu.make_async_copy(src.at[:, mine], dst.at[my_rows, :], own_sem.at[i])
        )
        own_copies[-1].start()

    small = ((ids_in, ids_ref), (order_in, order_ref), (long_in, long_ref))
    small += ((short_in, short_ref), (gain_in, gain_ref))
    small_copies = []
    for i, (src, dst) in enumerate(small):
        small_copies.append(pltpu.make_async_copy(src, dst, small_sem.at[i]))
        small_copies[-1].start()
    table_copies = []
    for j in range(units):
        cols = pl.ds(j * tile, tile)
        table_copies.append(
            pltpu.make_async_copy(
                table_ref.at[:, :, cols], table_buf.at[j], table_sem.at[j]
            )
        )
        table_copies[-1].start()

    pl.semaphore_wait(barrier, len(greet))

    pair_copies = []
    for i, (src, dst) in enumerate(pairs):
        pair_copies.append(
            pltpu.make_async_remote_copy(
                src_ref=src.at[:, theirs],
                dst_ref=dst.at[my_rows, :],
                send_sem=pair_send.at[i],
                recv_sem=pair_recv.at[i],
                device_id=(sibling, my_grp),
                device_id_type=MESH,
            )
        )
        pair_copies[-1].start()
    ids_copies = []
    for i in range(2):
        ids_copies.append(
            pltpu.make_async_remote_copy(
                src_ref=ids_in,
                dst_ref=ids_buf.at[i],
                send_sem=ids_send.at[i],
                recv_sem=ids_recv.at[i],
                device_id=(after[i], my_grp),
                device_id_type=MESH,
            )
        )
        ids_copies[-1].start()

    def ring_copy(to_right, is_key, step):
        buf = kbuf if is_key else vbuf
        if to_right:
            src, dst = step - 1, step
        else:
            src, dst = (chips - step + 1) % chips, chips - step
        slot = (0 if to_right else 1, 0 if is_key else 1, step - 1)
        return pltpu.make_async_remote_copy(
            src_ref=buf.at[src],
            dst_ref=buf.at[dst],
            send_sem=ring_send.at[slot],
            recv_sem=ring_recv.at[slot],
            device_id=(right if to_right else left, my_grp),
            device_id_type=MESH,
        )

    for i in range(2):
        own_copies[i].wait()
        pair_copies[i].wait_recv()
        ring_copy(True, i == 0, 1).start() if i == 0 or far > 1 else None
        ring_copy(False, i == 0, 1).start() if i == 1 or far > 1 else None

    def pass_on(step, first):
        last = step + 1 == far
        for to_right in (True, False):
            is_key = to_right == first
            ring_copy(to_right, is_key, step).wait_recv()
            if first or not last:
                ring_copy(to_right, is_key, step + 1).start()

    for copy in small_copies:
        copy.wait()

    anti = lax.broadcasted_iota(jnp.int32, (taps, rows + taps), 1) + lax.broadcasted_iota(
        jnp.int32, (taps, rows + taps), 0
    )
    anti = jnp.where(anti == taps, 1.0, 0.0).astype(BF16)
    taps_buf[...] = jnp.dot(long_ref[...], anti, preferred_element_type=F32)

    for copy in ids_copies:
        copy.wait_recv()
    first_row = me * rows

    def one_hot(row_ids, offset):
        down = jnp.transpose(jnp.broadcast_to(row_ids, (HD, rows)))
        spot = lax.broadcasted_iota(jnp.int32, (rows, HD), 0) + (first_row + offset)
        down = jnp.where(spot >= 0, down, -1)
        lane = lax.broadcasted_iota(jnp.int32, (rows, HD), 1)
        parts = [
            jnp.where(down == lane + b * HD, 1.0, 0.0).astype(BF16) for b in range(vocab // HD)
        ]
        return jnp.concatenate(parts, axis=1)

    hot[0:behind, :] = one_hot(ids_buf[1], -2 * rows)[rows - behind :, :]
    hot[behind : behind + rows, :] = one_hot(ids_buf[0], -rows)
    hot[behind + rows :, :] = one_hot(ids_ref[...], 0)

    tail = rows + 16

    def short_rows(feat, stream, base, count, lanes, cols):
        out = None
        for k in range(short_taps):
            term = short_ref[stream, pl.ds(k, 1), cols] * feat[
                pl.ds(base - k, count), lanes
            ]
            out = term if out is None else out + term
        return out

    def hyena_unit(j, done):
        table_copies[j].wait()
        feat_a[...] = jnp.dot(hot[...], table_buf[j, 1], preferred_element_type=F32)
        feat_c[...] = jnp.dot(hot[...], table_buf[j, 3], preferred_element_type=F32)
        feat_b[...] = jnp.dot(
            hot[lead - 16 :, :], table_buf[j, 2], preferred_element_type=F32
        )
        residual = jnp.dot(hot[lead:, :], table_buf[j, 0], preferred_element_type=F32)
        mixed[:, j * tile : (j + 1) * tile] = residual
        step_rows = 64
        for sub in range(tile // HD):
            lanes = slice(sub * HD, (sub + 1) * HD)
            cols = slice(j * tile + sub * HD, j * tile + (sub + 1) * HD)
            for r in range(0, taps + rows, step_rows):
                base = lead - taps + r
                one = short_rows(feat_a, 0, base, step_rows, lanes, cols)
                three = short_rows(feat_c, 2, base, step_rows, lanes, cols)
                prod[r : r + step_rows, lanes] = (one * three).astype(BF16)
        done()
        for sub in range(tile // HD):
            lanes = slice(sub * HD, (sub + 1) * HD)
            cols = slice(j * tile + sub * HD, j * tile + (sub + 1) * HD)
            block = prod[:, lanes]
            lane_group = lax.broadcasted_iota(jnp.int32, (rows, HD), 1) // group_size
            per_sub = HD // group_size
            first_group = (j * tile + sub * HD) // group_size

            def add_group(g, conv):
                line = taps_buf[pl.ds(first_group + g, 1), :]
                wide = jnp.broadcast_to(line, (rows, rows + taps))
                band = pltpu.roll(wide, 0, 1, stride=1, stride_axis=0).astype(BF16)
                part = jnp.dot(band, block, preferred_element_type=F32)
                return jnp.where(lane_group == g, part, conv)

            conv = lax.fori_loop(
                0, per_sub, add_group, jnp.zeros((rows, HD), F32), unroll=True
            )
            two = short_rows(feat_b, 1, 16, rows, lanes, cols)
            whole = mixed[:, cols] + two * conv
            mixed[:, cols] = whole
            square = whole * whole
            if j == 0 and sub == 0:
                squares[0] = square
            else:
                squares[0] = squares[0] + square

    def positions(of_chip, shape, dim):
        at = lax.broadcasted_iota(jnp.int32, shape, dim)
        piece = at // half_rows
        start = jnp.full(shape, order_ref[of_chip * 4], jnp.int32)
        for b in range(1, 4):
            start = jnp.where(piece == b, order_ref[of_chip * 4 + b], start)
        return start * half_rows + at % half_rows

    scale = 1.0 / math.sqrt(HD)

    def attend(slot, start):
        owner = chip_at(lax.rem(place + chips - slot, chips))
        key_pos = positions(owner, (1, 2 * rows), 1)
        query_pos = positions(chip, (2 * rows, 1), 0)
        visible = key_pos <= query_pos
        for head in range(heads):
            cols = slice(head * HD, (head + 1) * HD)
            scores = lax.dot_general(
                qbuf[:, cols],
                kbuf[slot, :, cols],
                (((1,), (1,)), ((), ())),
                preferred_element_type=F32,
            )
            scores = jnp.where(visible, scores * scale, neg_fill)
            top = jnp.max(scores, axis=1, keepdims=True)
            if not start:
                old = peak[head]
                top = jnp.maximum(old, top)
            weights = jnp.where(visible, jnp.exp(scores - top), 0.0)
            mass = jnp.sum(weights, axis=1, keepdims=True)
            summed = jnp.dot(
                weights.astype(BF16), vbuf[slot, :, cols], preferred_element_type=F32
            )
            if not start:
                shrink = jnp.exp(old - top)
                mass = total[head] * shrink + mass
                summed = acc[head] * shrink + summed
            peak[head] = top
            total[head] = mass
            acc[head] = summed

    events = [(s, f) for s in range(1, far) for f in (True, False)]
    passed = []

    def next_event():
        if events:
            step, first = events.pop(0)
            pass_on(step, first)
            if not first:
                passed.append(step)

    def nothing():
        return None

    for j in range(units):
        hyena_unit(j, next_event if j % 2 == 0 else nothing)

    sq_copies = []
    for i, g in enumerate(peers):
        sq_copies.append(
            pltpu.make_async_remote_copy(
                src_ref=squares.at[0],
                dst_ref=squares.at[i + 1],
                send_sem=sq_send.at[i],
                recv_sem=sq_recv.at[i],
                device_id=(me, g),
                device_id_type=MESH,
            )
        )
        sq_copies[-1].start()

    next_event()
    own_copies[2].wait()
    pair_copies[2].wait_recv()
    attend(0, True)
    while events:
        for step in passed:
            attend(step, False)
            attend(chips - step, False)
        passed.clear()
        next_event()

    for copy in sq_copies:
        copy.wait_recv()
    sum_sq = squares[0]
    for i in range(len(peers)):
        sum_sq = sum_sq + squares[i + 1]
    mean = jnp.sum(sum_sq, axis=1, keepdims=True) / (channels * n_grp)
    inverse = lax.rsqrt(mean + eps_norm)
    hy_ref[...] = (mixed[...] * gain_ref[...] * inverse).astype(BF16)
    for step in passed:
        attend(step, False)
        attend(chips - step, False)

    ring_copy(True, True, far).wait_recv()
    ring_copy(False, False, far).wait_recv()
    attend(far, False)

    for head in range(heads):
        cols = slice(head * HD, (head + 1) * HD)
        obuf[:, cols] = (acc[head] / total[head]).astype(BF16)
    their_rows = pl.ds(pl.multiple_of((1 - core) * rows, rows), rows)
    back = pltpu.make_async_remote_copy(
        src_ref=obuf.at[their_rows, :],
        dst_ref=oland,
        send_sem=out_send,
        recv_sem=out_recv,
        device_id=(sibling, my_grp),
        device_id_type=MESH,
    )
    back.start()
    for copy in pair_copies + ids_copies + sq_copies:
        copy.wait_send()
    for step in range(1, far + 1):
        for to_right in (True, False):
            for is_key in (True, False):
                if step < far or to_right == is_key:
                    ring_copy(to_right, is_key, step).wait_send()
    kept = obuf[my_rows, :]
    back.wait()
    got = oland[...]
    att_ref[:, :half_width] = jnp.where(core == 0, kept, got)
    att_ref[:, half_width:] = jnp.where(core == 0, got, kept)


def body(
    n_ctx,
    n_grp,
    queries,
    keys,
    values,
    block_order,
    token_ids,
    stream_table,
    short_filter,
    long_filter,
    norm_gain,
):
    rows, width = queries.shape
    half_width = width // 2
    heads = half_width // HD
    channels = stream_table.shape[2]
    vocab = stream_table.shape[1]
    groups, taps = long_filter.shape
    lead = ceil_to(taps - 1 + short_filter.shape[1] - 1, 16)
    tile = math.gcd(channels, 256)
    units = channels // tile
    chips = n_ctx // 2
    far = chips // 2
    vmem = pl.BlockSpec(memory_space=pltpu.VMEM)
    dma = pltpu.SemaphoreType.DMA
    return pl.pallas_call(
        functools.partial(kernel, (n_ctx, n_grp, tile)),
        out_shape=(
            jax.ShapeDtypeStruct((rows, width), BF16),
            jax.ShapeDtypeStruct((rows, channels), BF16),
        ),
        in_specs=[pl.BlockSpec(memory_space=pltpu.HBM)] * 9,
        out_specs=(vmem, vmem),
        scratch_shapes=[
            pltpu.SMEM(block_order.shape, jnp.int32),
            pltpu.VMEM((1, rows), jnp.int32),
            pltpu.VMEM(short_filter.shape, F32),
            pltpu.VMEM(long_filter.shape, BF16),
            pltpu.VMEM((1, channels), F32),
            dma((5,)),
            pltpu.VMEM((chips, 2 * rows, half_width), BF16),
            pltpu.VMEM((chips, 2 * rows, half_width), BF16),
            pltpu.VMEM((2 * rows, half_width), BF16),
            pltpu.VMEM((2 * rows, half_width), BF16),
            pltpu.VMEM((rows, half_width), BF16),
            pltpu.VMEM((2, 1, rows), jnp.int32),
            pltpu.VMEM((units, 4, vocab, tile), BF16),
            pltpu.VMEM((lead + rows, vocab), BF16),
            pltpu.VMEM((lead + rows, tile), F32),
            pltpu.VMEM((rows + 16, tile), F32),
            pltpu.VMEM((lead + rows, tile), F32),
            pltpu.VMEM((rows + taps, tile), BF16),
            pltpu.VMEM((groups, rows + taps), F32),
            pltpu.VMEM((rows, channels), F32),
            pltpu.VMEM((n_grp, rows, HD), F32),
            pltpu.VMEM((heads, 2 * rows, 1), F32),
            pltpu.VMEM((heads, 2 * rows, 1), F32),
            pltpu.VMEM((heads, 2 * rows, HD), F32),
            dma((3,)),
            dma((3,)),
            dma((3,)),
            dma((2,)),
            dma((2,)),
            dma((2, 2, far)),
            dma((2, 2, far)),
            dma((units,)),
            dma((max(n_grp - 1, 1),)),
            dma((max(n_grp - 1, 1),)),
            dma,
            dma,
        ],
        compiler_params=pltpu.CompilerParams(
            collective_id=0, has_side_effects=True, vmem_limit_bytes=64 * 1024 * 1024
        ),
    )(
        block_order,
        queries,
        keys,
        values,
        token_ids.reshape(1, rows),
        stream_table,
        short_filter,
        long_filter,
        norm_gain.reshape(1, channels),
    )


def solution(mesh):
    placed = (
        P("ctx", "grp"),
        P("ctx", "grp"),
        P("ctx", "grp"),
        P(),
        P("ctx"),
        P(None, None, "grp"),
        P(None, None, "grp"),
        P("grp", None),
        P("grp"),
    )
    return jax.shard_map(
        functools.partial(body, mesh.shape["ctx"], mesh.shape["grp"]),
        mesh=mesh,
        in_specs=placed,
        out_specs=(P("ctx", "grp"), P("ctx", "grp")),
        check_vma=False,
    )
```

```python
import functools
import math

import jax
import jax.numpy as jnp
from jax import lax
from jax.experimental import pallas as pl
from jax.experimental.pallas import tpu as pltpu
from jax.sharding import PartitionSpec as P

HD = 128
MESH = pl.DeviceIdType.MESH
neg_fill = -1e30
eps_norm = 1e-06
F32 = jnp.float32
BF16 = jnp.bfloat16


def ceil_to(value, unit):
    return -(-value // unit) * unit


def kernel(
    sizes,
    order_in,
    q_ref,
    k_ref,
    v_ref,
    ids_in,
    table_ref,
    short_in,
    long_in,
    gain_in,
    att_ref,
    hy_ref,
    order_ref,
    ids_ref,
    short_ref,
    long_ref,
    gain_ref,
    small_sem,
    kbuf,
    vbuf,
    qbuf,
    obuf,
    oland,
    ids_buf,
    table_buf,
    hot,
    feat_a,
    feat_b,
    feat_c,
    prod,
    taps_buf,
    mixed,
    squares,
    peak,
    total,
    acc,
    own_sem,
    pair_send,
    pair_recv,
    ids_send,
    ids_recv,
    ring_send,
    ring_recv,
    table_sem,
    sq_send,
    sq_recv,
    out_send,
    out_recv,
):
    n_ctx, n_grp, tile = sizes
    rows, width = q_ref.shape
    half_width = width // 2
    heads = half_width // HD
    half_rows = rows // 2
    channels = table_ref.shape[2]
    vocab = table_ref.shape[1]
    short_taps = short_ref.shape[1]
    groups, taps = long_ref.shape
    group_size = channels // groups
    units = channels // tile
    lead = hot.shape[0] - rows
    behind = lead - rows
    chips = n_ctx // 2
    far = chips // 2

    me = lax.axis_index("ctx")
    my_grp = lax.axis_index("grp")
    chip = me // 2
    core = me % 2

    def ring_of(c):
        return jnp.where(c % 2 == 0, c // 2, chips - 1 - c // 2)

    def chip_at(place):
        return jnp.where(place < far, 2 * place, 2 * (chips - 1 - place) + 1)

    place = ring_of(chip)
    sibling = chip * 2 + (1 - core)
    right = chip_at(lax.rem(place + 1, chips)) * 2 + core
    left = chip_at(lax.rem(place + chips - 1, chips)) * 2 + core
    after = [lax.rem(me + d, n_ctx) for d in (1, 2)]
    before = [lax.rem(me + n_ctx - d, n_ctx) for d in (1, 2)]
    peers = [lax.rem(my_grp + d, n_grp) for d in range(1, n_grp)]

    barrier = pltpu.get_barrier_semaphore()
    greet = [(t, my_grp) for t in [sibling, right, left] + after + before]
    greet += [(me, g) for g in peers]
    for target in greet:
        pl.semaphore_signal(barrier, inc=1, device_id=target, device_id_type=MESH)

    mine = pl.ds(pl.multiple_of(core * half_width, half_width), half_width)
    theirs = pl.ds(pl.multiple_of((1 - core) * half_width, half_width), half_width)
    my_rows = pl.ds(pl.multiple_of(core * rows, rows), rows)
    pairs = ((k_ref, kbuf.at[0]), (v_ref, vbuf.at[0]), (q_ref, qbuf))
    own_copies = []
    for i, (src, dst) in enumerate(pairs):
        own_copies.append(
            pltpu.make_async_copy(src.at[:, mine], dst.at[my_rows, :], own_sem.at[i])
        )
        own_copies[-1].start()

    small = ((ids_in, ids_ref), (order_in, order_ref), (long_in, long_ref))
    small += ((short_in, short_ref), (gain_in, gain_ref))
    small_copies = []
    for i, (src, dst) in enumerate(small):
        small_copies.append(pltpu.make_async_copy(src, dst, small_sem.at[i]))
        small_copies[-1].start()
    table_copies = []
    for j in range(units):
        cols = pl.ds(j * tile, tile)
        table_copies.append(
            pltpu.make_async_copy(
                table_ref.at[:, :, cols], table_buf.at[j], table_sem.at[j]
            )
        )
        table_copies[-1].start()

    pl.semaphore_wait(barrier, len(greet))

    pair_copies = []
    for i, (src, dst) in enumerate(pairs):
        pair_copies.append(
            pltpu.make_async_remote_copy(
                src_ref=src.at[:, theirs],
                dst_ref=dst.at[my_rows, :],
                send_sem=pair_send.at[i],
                recv_sem=pair_recv.at[i],
                device_id=(sibling, my_grp),
                device_id_type=MESH,
            )
        )
        pair_copies[-1].start()
    ids_copies = []
    for i in range(2):
        ids_copies.append(
            pltpu.make_async_remote_copy(
                src_ref=ids_in,
                dst_ref=ids_buf.at[i],
                send_sem=ids_send.at[i],
                recv_sem=ids_recv.at[i],
                device_id=(after[i], my_grp),
                device_id_type=MESH,
            )
        )
        ids_copies[-1].start()

    their_half = pl.ds(pl.multiple_of((1 - core) * rows, rows), rows)
    halves = (my_rows, their_half)

    def ring_copy(to_right, is_key, step, half):
        buf = kbuf if is_key else vbuf
        if to_right:
            src, dst = step - 1, step
        else:
            src, dst = (chips - step + 1) % chips, chips - step
        slot = (0 if to_right else 1, 0 if is_key else 1, 2 * (step - 1) + half)
        return pltpu.make_async_remote_copy(
            src_ref=buf.at[src, halves[half], :],
            dst_ref=buf.at[dst, halves[half], :],
            send_sem=ring_send.at[slot],
            recv_sem=ring_recv.at[slot],
            device_id=(right if to_right else left, my_grp),
            device_id_type=MESH,
        )

    def send_on(to_right, is_key, step, half):
        if step < far or to_right == is_key:
            ring_copy(to_right, is_key, step, half).start()

    for half in range(2):
        for i in range(2):
            if half == 0:
                own_copies[i].wait()
            else:
                pair_copies[i].wait_recv()
            send_on(True, i == 0, 1, half)
            send_on(False, i == 0, 1, half)

    def pass_on(step, half):
        for order in (0, 1):
            for to_right in (True, False):
                is_key = to_right == (order == 0)
                ring_copy(to_right, is_key, step, half).wait_recv()
                send_on(to_right, is_key, step + 1, half)

    for copy in small_copies:
        copy.wait()

    anti = lax.broadcasted_iota(jnp.int32, (taps, rows + taps), 1) + lax.broadcasted_iota(
        jnp.int32, (taps, rows + taps), 0
    )
    anti = jnp.where(anti == taps, 1.0, 0.0).astype(BF16)
    taps_buf[...] = jnp.dot(long_ref[...], anti, preferred_element_type=F32)

    for copy in ids_copies:
        copy.wait_recv()
    first_row = me * rows

    def one_hot(row_ids, offset):
        down = jnp.transpose(jnp.broadcast_to(row_ids, (HD, rows)))
        spot = lax.broadcasted_iota(jnp.int32, (rows, HD), 0) + (first_row + offset)
        down = jnp.where(spot >= 0, down, -1)
        lane = lax.broadcasted_iota(jnp.int32, (rows, HD), 1)
        parts = [
            jnp.where(down == lane + b * HD, 1.0, 0.0).astype(BF16) for b in range(vocab // HD)
        ]
        return jnp.concatenate(parts, axis=1)

    hot[0:behind, :] = one_hot(ids_buf[1], -2 * rows)[rows - behind :, :]
    hot[behind : behind + rows, :] = one_hot(ids_buf[0], -rows)
    hot[behind + rows :, :] = one_hot(ids_ref[...], 0)

    tail = rows + 16

    def short_rows(feat, stream, base, count, lanes, cols):
        out = None
        for k in range(short_taps):
            term = short_ref[stream, pl.ds(k, 1), cols] * feat[
                pl.ds(base - k, count), lanes
            ]
            out = term if out is None else out + term
        return out

    def hyena_unit(j, done):
        table_copies[j].wait()
        feat_a[...] = jnp.dot(hot[...], table_buf[j, 1], preferred_element_type=F32)
        feat_c[...] = jnp.dot(hot[...], table_buf[j, 3], preferred_element_type=F32)
        feat_b[...] = jnp.dot(
            hot[lead - 16 :, :], table_buf[j, 2], preferred_element_type=F32
        )
        residual = jnp.dot(hot[lead:, :], table_buf[j, 0], preferred_element_type=F32)
        mixed[:, j * tile : (j + 1) * tile] = residual
        step_rows = 64
        for sub in range(tile // HD):
            lanes = slice(sub * HD, (sub + 1) * HD)
            cols = slice(j * tile + sub * HD, j * tile + (sub + 1) * HD)
            for r in range(0, taps + rows, step_rows):
                base = lead - taps + r
                one = short_rows(feat_a, 0, base, step_rows, lanes, cols)
                three = short_rows(feat_c, 2, base, step_rows, lanes, cols)
                prod[r : r + step_rows, lanes] = (one * three).astype(BF16)
        done()
        for sub in range(tile // HD):
            lanes = slice(sub * HD, (sub + 1) * HD)
            cols = slice(j * tile + sub * HD, j * tile + (sub + 1) * HD)
            block = prod[:, lanes]
            lane_group = lax.broadcasted_iota(jnp.int32, (rows, HD), 1) // group_size
            per_sub = HD // group_size
            first_group = (j * tile + sub * HD) // group_size

            def add_group(g, conv):
                line = taps_buf[pl.ds(first_group + g, 1), :]
                wide = jnp.broadcast_to(line, (rows, rows + taps))
                band = pltpu.roll(wide, 0, 1, stride=1, stride_axis=0).astype(BF16)
                part = jnp.dot(band, block, preferred_element_type=F32)
                return jnp.where(lane_group == g, part, conv)

            conv = lax.fori_loop(
                0, per_sub, add_group, jnp.zeros((rows, HD), F32), unroll=True
            )
            two = short_rows(feat_b, 1, 16, rows, lanes, cols)
            whole = mixed[:, cols] + two * conv
            mixed[:, cols] = whole
            square = whole * whole
            if j == 0 and sub == 0:
                squares[0] = square
            else:
                squares[0] = squares[0] + square

    def positions(of_chip, shape, dim):
        at = lax.broadcasted_iota(jnp.int32, shape, dim)
        piece = at // half_rows
        start = jnp.full(shape, order_ref[of_chip * 4], jnp.int32)
        for b in range(1, 4):
            start = jnp.where(piece == b, order_ref[of_chip * 4 + b], start)
        return start * half_rows + at % half_rows

    scale = 1.0 / math.sqrt(HD)

    def attend(slot, start):
        owner = chip_at(lax.rem(place + chips - slot, chips))
        key_pos = positions(owner, (1, 2 * rows), 1)
        query_pos = positions(chip, (2 * rows, 1), 0)
        visible = key_pos <= query_pos
        for head in range(heads):
            cols = slice(head * HD, (head + 1) * HD)
            scores = lax.dot_general(
                qbuf[:, cols],
                kbuf[slot, :, cols],
                (((1,), (1,)), ((), ())),
                preferred_element_type=F32,
            )
            scores = jnp.where(visible, scores * scale, neg_fill)
            top = jnp.max(scores, axis=1, keepdims=True)
            if not start:
                old = peak[head]
                top = jnp.maximum(old, top)
            weights = jnp.where(visible, jnp.exp(scores - top), 0.0)
            mass = jnp.sum(weights, axis=1, keepdims=True)
            summed = jnp.dot(
                weights.astype(BF16), vbuf[slot, :, cols], preferred_element_type=F32
            )
            if not start:
                shrink = jnp.exp(old - top)
                mass = total[head] * shrink + mass
                summed = acc[head] * shrink + summed
            peak[head] = top
            total[head] = mass
            acc[head] = summed

    events = [(s, f) for s in range(1, far) for f in (0, 1)]
    passed = []

    def next_event():
        if events:
            step, first = events.pop(0)
            pass_on(step, first)
            if first:
                passed.append(step)

    def nothing():
        return None

    for j in range(units):
        hyena_unit(j, next_event if j % 2 == 0 else nothing)

    sq_copies = []
    for i, g in enumerate(peers):
        sq_copies.append(
            pltpu.make_async_remote_copy(
                src_ref=squares.at[0],
                dst_ref=squares.at[i + 1],
                send_sem=sq_send.at[i],
                recv_sem=sq_recv.at[i],
                device_id=(me, g),
                device_id_type=MESH,
            )
        )
        sq_copies[-1].start()

    next_event()
    own_copies[2].wait()
    pair_copies[2].wait_recv()
    attend(0, True)
    while events:
        for step in passed:
            attend(step, False)
            attend(chips - step, False)
        passed.clear()
        next_event()

    for copy in sq_copies:
        copy.wait_recv()
    sum_sq = squares[0]
    for i in range(len(peers)):
        sum_sq = sum_sq + squares[i + 1]
    mean = jnp.sum(sum_sq, axis=1, keepdims=True) / (channels * n_grp)
    inverse = lax.rsqrt(mean + eps_norm)
    hy_ref[...] = (mixed[...] * gain_ref[...] * inverse).astype(BF16)
    for step in passed:
        attend(step, False)
        attend(chips - step, False)

    for half in range(2):
        ring_copy(True, True, far, half).wait_recv()
        ring_copy(False, False, far, half).wait_recv()
    attend(far, False)

    for head in range(heads):
        cols = slice(head * HD, (head + 1) * HD)
        obuf[:, cols] = (acc[head] / total[head]).astype(BF16)
    their_rows = pl.ds(pl.multiple_of((1 - core) * rows, rows), rows)
    back = pltpu.make_async_remote_copy(
        src_ref=obuf.at[their_rows, :],
        dst_ref=oland,
        send_sem=out_send,
        recv_sem=out_recv,
        device_id=(sibling, my_grp),
        device_id_type=MESH,
    )
    back.start()
    for copy in pair_copies + ids_copies + sq_copies:
        copy.wait_send()
    for step in range(1, far + 1):
        for to_right in (True, False):
            for is_key in (True, False):
                if step < far or to_right == is_key:
                    for half in range(2):
                        ring_copy(to_right, is_key, step, half).wait_send()
    kept = obuf[my_rows, :]
    back.wait()
    got = oland[...]
    att_ref[:, :half_width] = jnp.where(core == 0, kept, got)
    att_ref[:, half_width:] = jnp.where(core == 0, got, kept)


def body(
    n_ctx,
    n_grp,
    queries,
    keys,
    values,
    block_order,
    token_ids,
    stream_table,
    short_filter,
    long_filter,
    norm_gain,
):
    rows, width = queries.shape
    half_width = width // 2
    heads = half_width // HD
    channels = stream_table.shape[2]
    vocab = stream_table.shape[1]
    groups, taps = long_filter.shape
    lead = ceil_to(taps - 1 + short_filter.shape[1] - 1, 16)
    tile = math.gcd(channels, 256)
    units = channels // tile
    chips = n_ctx // 2
    far = chips // 2
    vmem = pl.BlockSpec(memory_space=pltpu.VMEM)
    dma = pltpu.SemaphoreType.DMA
    return pl.pallas_call(
        functools.partial(kernel, (n_ctx, n_grp, tile)),
        out_shape=(
            jax.ShapeDtypeStruct((rows, width), BF16),
            jax.ShapeDtypeStruct((rows, channels), BF16),
        ),
        in_specs=[pl.BlockSpec(memory_space=pltpu.HBM)] * 9,
        out_specs=(vmem, vmem),
        scratch_shapes=[
            pltpu.SMEM(block_order.shape, jnp.int32),
            pltpu.VMEM((1, rows), jnp.int32),
            pltpu.VMEM(short_filter.shape, F32),
            pltpu.VMEM(long_filter.shape, BF16),
            pltpu.VMEM((1, channels), F32),
            dma((5,)),
            pltpu.VMEM((chips, 2 * rows, half_width), BF16),
            pltpu.VMEM((chips, 2 * rows, half_width), BF16),
            pltpu.VMEM((2 * rows, half_width), BF16),
            pltpu.VMEM((2 * rows, half_width), BF16),
            pltpu.VMEM((rows, half_width), BF16),
            pltpu.VMEM((2, 1, rows), jnp.int32),
            pltpu.VMEM((units, 4, vocab, tile), BF16),
            pltpu.VMEM((lead + rows, vocab), BF16),
            pltpu.VMEM((lead + rows, tile), F32),
            pltpu.VMEM((rows + 16, tile), F32),
            pltpu.VMEM((lead + rows, tile), F32),
            pltpu.VMEM((rows + taps, tile), BF16),
            pltpu.VMEM((groups, rows + taps), F32),
            pltpu.VMEM((rows, channels), F32),
            pltpu.VMEM((n_grp, rows, HD), F32),
            pltpu.VMEM((heads, 2 * rows, 1), F32),
            pltpu.VMEM((heads, 2 * rows, 1), F32),
            pltpu.VMEM((heads, 2 * rows, HD), F32),
            dma((3,)),
            dma((3,)),
            dma((3,)),
            dma((2,)),
            dma((2,)),
            dma((2, 2, 2 * far)),
            dma((2, 2, 2 * far)),
            dma((units,)),
            dma((max(n_grp - 1, 1),)),
            dma((max(n_grp - 1, 1),)),
            dma,
            dma,
        ],
        compiler_params=pltpu.CompilerParams(
            collective_id=0, has_side_effects=True, vmem_limit_bytes=64 * 1024 * 1024
        ),
    )(
        block_order,
        queries,
        keys,
        values,
        token_ids.reshape(1, rows),
        stream_table,
        short_filter,
        long_filter,
        norm_gain.reshape(1, channels),
    )


def solution(mesh):
    placed = (
        P("ctx", "grp"),
        P("ctx", "grp"),
        P("ctx", "grp"),
        P(),
        P("ctx"),
        P(None, None, "grp"),
        P(None, None, "grp"),
        P("grp", None),
        P("grp"),
    )
    return jax.shard_map(
        functools.partial(body, mesh.shape["ctx"], mesh.shape["grp"]),
        mesh=mesh,
        in_specs=placed,
        out_specs=(P("ctx", "grp"), P("ctx", "grp")),
        check_vma=False,
    )
```
